32 devices in a mesh: leaf: 4 (over y, x), row: 4 (over z), col: 2 (over core).
Axes of the slice: x: 2, y: 2, z: 4, core: 2. Of those that a mesh axis runs over, the one named last changes fastest.
Arguments:
- rhs_leaf: bfloat16 [4, 12288, 256], P('leaf', 'col'), may hold values from -6 to 6
- rhs_parent: bfloat16 [16384, 256], P(('leaf', 'row', 'col')), may hold values from -6 to 6
- inv_leaf: bfloat16 [4, 12288, 12288], P('leaf', 'row', 'col'), as said below
- panel: bfloat16 [4, 6144, 12288], P('leaf', 'col', 'row'), may hold values from -0.0546875 to 0.0546875
- row_map: int32 [4, 6144], P('leaf', 'col'), may hold values from 0 to 16383, as said below
- inv_parent: bfloat16 [16384, 16384], P(('row', 'col'), 'leaf'), as said below
Outputs:
- sol_leaf: bfloat16 [4, 12288, 256], P('leaf', 'col')
- sol_parent: bfloat16 [16384, 256], P(('leaf', 'row', 'col'))
The draws below stay inside these ranges and needn't reach their ends.
Inputs may be any that keep to these rules, and one draw needn't show every extreme that they name: Within one leaf the 6144 entries of row_map are distinct parent rows. Split the parent rows into 32 owner blocks of 16384 // 32 consecutive rows: in each aligned block of 768 consecutive entries of a leaf, at most 24 entries fall in one owner block, and exactly 24 in some. `inv_leaf`: lower triangular: zeros above the diagonal, diagonal entries between 0.5 and 2. `inv_parent`: lower triangular: zeros above the diagonal, diagonal entries between 0.5 and 2.
All inputs are finite; a program needn't handle non-finite values.
Results may differ from the reference program's by a relative error of at most 0.01.
Values may be sent and summed in bfloat16 or wider, within the bound.
No kernel may reach another device: no remote copies, remote signals or barrier semaphores. Data moves between devices by JAX's collectives and lax.ppermute only.
A program may use at most 192 MiB of HBM per device.

```python
import jax
import jax.numpy as jnp

NL = 12288
NA = 6144
NP = 16384
R = 256
LEAVES = 4
DEVICES = 32


def triangle(key, order):
    lower_key, diag_key = jax.random.split(key)
    rows = jnp.arange(order)[:, None]
    cols = jnp.arange(order)[None, :]
    entries = jax.random.normal(lower_key, (order, order), jnp.float32)
    entries = entries * order ** (-0.5)
    diagonal = jax.random.uniform(diag_key, (order,), jnp.float32, 0.5, 2.0)
    lower = jnp.where(cols < rows, entries, 0.0)
    return lower + jnp.where(cols == rows, diagonal[:, None], 0.0)


def draw_inv_leaf(key, part):
    blocks = [triangle(jax.random.fold_in(key, member), NL) for member in range(LEAVES)]
    return jnp.stack(blocks).astype(jnp.bfloat16)


def draw_inv_parent(key, part):
    return triangle(jax.random.fold_in(key, 77), NP).astype(jnp.bfloat16)


def leaf_map(key, member):
    owned = NP // DEVICES
    owners = jax.random.permutation(jax.random.fold_in(key, member), DEVICES)
    offsets = jax.random.randint(jax.random.fold_in(key, 1000 + member), (DEVICES,), 0, owned)
    position = jnp.arange(NA)
    owner_index = owners[position % DEVICES]
    local_row = (position // DEVICES + offsets[owner_index]) % owned
    return owner_index * owned + local_row


def draw_row_map(key, part):
    maps = [leaf_map(key, member) for member in range(LEAVES)]
    return jnp.stack(maps).astype(jnp.int32)


def block_levels(key, shape, shards, low, largest):
    gain, own = 1.0, jax.random.fold_in(key, 6)
    for axis_at, blocks in shards:
        draws = jnp.exp(jax.random.uniform(jax.random.fold_in(own, axis_at), (blocks,), jnp.float32, low / len(shards), largest / len(shards)))
        gain = gain * jnp.repeat(draws, shape[axis_at] // blocks).reshape([-1 if axis == axis_at else 1 for axis in range(len(shape))])
    return gain


def gaussian(own_key, dims, deviation, limit, shards=(), held_as=jnp.bfloat16):
    values = jax.random.normal(own_key, dims, jnp.float32) * deviation
    if len(shards) > 0:
        values = block_levels(own_key, dims, shards, -0.22, 0.18) * values
    return jnp.clip(values, min=-limit, max=limit).astype(held_as)


def setup_inputs(seed: int = 0) -> dict:
    keys = jax.random.split(jax.random.key(seed), 7)
    return {
        "rhs_leaf": gaussian(keys[0], (LEAVES, NL, R), 1.0, 6.0, ((0, 4), (1, 2))),
        "rhs_parent": gaussian(keys[1], (NP, R), 1.0, 6.0, ((0, 32),)),
        "inv_leaf": draw_inv_leaf(jax.random.fold_in(keys[6], 71), 0),
        "panel": gaussian(keys[3], (LEAVES, NA, NL), NL ** -0.5, 0.0546875, ((0, 4), (1, 2), (2, 4))),
        "row_map": draw_row_map(jax.random.fold_in(keys[6], 71), 0),
        "inv_parent": draw_inv_parent(jax.random.fold_in(keys[6], 71), 0),
    }


def reference(rhs_leaf, rhs_parent, inv_leaf, panel, row_map, inv_parent):
    forward = []
    acc = rhs_parent.astype(jnp.float32)
    for member in range(LEAVES):
        solved = jnp.dot(inv_leaf[member], rhs_leaf[member], preferred_element_type=jnp.float32).astype(jnp.bfloat16)
        forward.append(solved)
        update = jnp.dot(panel[member], solved, preferred_element_type=jnp.float32)
        acc = acc.at[row_map[member]].add(-update)
    reduced = acc.astype(jnp.bfloat16)
    fwd_parent = jnp.dot(inv_parent, reduced, preferred_element_type=jnp.float32).astype(jnp.bfloat16)
    sol_parent = jnp.dot(inv_parent.T, fwd_parent, preferred_element_type=jnp.float32).astype(jnp.bfloat16)
    results = []
    for member in range(LEAVES):
        picked = sol_parent[row_map[member]]
        coupling = jnp.dot(panel[member].T, picked, preferred_element_type=jnp.float32)
        corrected = (forward[member].astype(jnp.float32) - coupling).astype(jnp.bfloat16)
        results.append(jnp.dot(inv_leaf[member].T, corrected, preferred_element_type=jnp.float32).astype(jnp.bfloat16))
    return jnp.stack(results), sol_parent
```

```python
import jax
import jax.numpy as jnp
from jax import lax
from jax.sharding import PartitionSpec as P

ALL = ("leaf", "row", "col")
F32 = jnp.float32
BF16 = jnp.bfloat16
CHUNKS = 8


def matmul(a, x):
    return jnp.dot(a, x, preferred_element_type=F32)


def matmul_t(a, x):
    return lax.dot_general(a, x, (((0,), (0,)), ((), ())), preferred_element_type=F32)


def sum_cores(part):
    if lax.axis_size("col") == 2:
        other = lax.ppermute(part.astype(BF16), "col", [(0, 1), (1, 0)])
        return part + other.astype(F32)
    return lax.psum(part, "col")


def sum_leaves(part):
    size = lax.axis_size("leaf")
    bits = [1 << b for b in range(size.bit_length() - 1)]
    halves = jnp.split(part, 2, axis=0)
    orders = (bits, bits[::-1])
    for step in range(len(bits)):
        moved = [
            lax.ppermute(h.astype(BF16), "leaf", [(i, i ^ order[step]) for i in range(size)])
            for h, order in zip(halves, orders)
        ]
        halves = [h + m.astype(F32) for h, m in zip(halves, moved)]
    return jnp.concatenate(halves, axis=0).astype(BF16)


def gather_block(own):
    rows, cols = own.shape
    depth = lax.axis_size("row")
    z = lax.axis_index("row")
    parts = [own]
    for d in range(1, depth):
        parts.append(lax.ppermute(own, "row", [(i, (i + d) % depth) for i in range(depth)]))
    stacked = jnp.stack(parts)
    placed = jnp.take(stacked, (z - jnp.arange(depth)) % depth, axis=0, mode="clip")
    cores = lax.axis_size("col")
    if cores == 2:
        c = lax.axis_index("col")
        other = lax.ppermute(placed, "col", [(0, 1), (1, 0)])
        both = jnp.stack(
            [jnp.where(c == 0, placed, other), jnp.where(c == 0, other, placed)], axis=1
        )
    else:
        both = lax.all_gather(placed, "col", axis=1)
    return both.reshape(depth * cores * rows, cols)


def scatter_block(part):
    depth = lax.axis_size("row")
    cores = lax.axis_size("col")
    z = lax.axis_index("row")
    rows = part.shape[0] // (depth * cores)
    split = part.reshape(depth, cores, rows, part.shape[1])
    if cores == 2:
        c = lax.axis_index("col")
        mine = lax.dynamic_index_in_dim(split, c, 1, keepdims=False)
        theirs = lax.dynamic_index_in_dim(split, 1 - c, 1, keepdims=False).astype(BF16)
        summed = mine + lax.ppermute(theirs, "col", [(0, 1), (1, 0)]).astype(F32)
    else:
        summed = lax.psum_scatter(split, "col", scatter_dimension=1, tiled=True)[:, 0]
    total = lax.dynamic_index_in_dim(summed, z, 0, keepdims=False)
    summed = summed.astype(BF16)
    for d in range(1, depth):
        chunk = lax.dynamic_index_in_dim(summed, (z + d) % depth, 0, keepdims=False)
        moved = lax.ppermute(chunk, "row", [(i, (i + d) % depth) for i in range(depth)])
        total = total + moved.astype(F32)
    return total.astype(BF16)


def sum_rows(part):
    depth = lax.axis_size("row")
    z = lax.axis_index("row")
    size = part.shape[0] // CHUNKS
    down = [(i + 1, i) for i in range(depth - 1)]
    up = [(i, i + 1) for i in range(depth - 1)]

    def chunk(array, j):
        return lax.dynamic_slice_in_dim(array, jnp.clip(j, 0, CHUNKS - 1) * size, size, 0)

    def add(array, j, moved):
        old = chunk(array, j)
        new = jnp.where((j >= 0) & (j < CHUNKS), old + moved, old)
        return lax.dynamic_update_slice_in_dim(array, new, jnp.clip(j, 0, CHUNKS - 1) * size, 0)

    total = part
    from_above = jnp.zeros((size, part.shape[1]), BF16)
    from_below = from_above
    for step in range(CHUNKS + depth - 2):
        send_down = chunk(part, step - (depth - 1) + z) + from_above
        send_up = chunk(part, step - z) + from_below
        from_above = lax.ppermute(send_down, "row", down)
        from_below = lax.ppermute(send_up, "row", up)
        total = add(total, step - depth + 2 + z, from_above)
        total = add(total, step - z + 1, from_below)
    return total


def slots_of(row_map, own, devices, depth):
    blocks = row_map.reshape(depth, -1)
    size = blocks.shape[1]
    cap = -(-size // devices)
    owner = blocks // own
    earlier = jnp.arange(size)[None, :] < jnp.arange(size)[:, None]
    rank = jnp.sum((owner[:, :, None] == owner[:, None, :]) & earlier[None], axis=2, dtype=jnp.int32)
    slot = owner * cap + rank
    hit = slot[:, None, :] == jnp.arange(devices * cap, dtype=jnp.int32)[None, :, None]
    local = jnp.max(jnp.where(hit, (blocks % own)[:, None, :], -1), axis=2)
    local = local.reshape(depth, devices, cap).transpose(1, 0, 2).reshape(devices, depth * cap)
    return hit.astype(BF16), local


def per_device(rhs_leaf, rhs_parent, inv_leaf, panel, row_map, inv_parent):
    leaves, depth, cores = (lax.axis_size(a) for a in ALL)
    devices = leaves * depth * cores
    me = lax.axis_index(ALL)
    own, width = rhs_parent.shape

    pick, local = slots_of(row_map[0], own, devices, depth)
    per_owner = local.shape[1]
    cap = per_owner // depth
    lists = lax.all_gather(local, ("leaf", "col"))
    mine = lax.dynamic_index_in_dim(lists, me, 1, keepdims=False).reshape(-1)
    place = (mine[None, :] == jnp.arange(own, dtype=jnp.int32)[:, None]).astype(BF16)

    forward = sum_cores(matmul(inv_leaf[0], rhs_leaf[0])).astype(BF16)
    update = matmul(panel[0], forward).astype(BF16).reshape(depth, -1, width)
    packed = jnp.einsum("bsi,bir->bsr", pick, update, preferred_element_type=F32).astype(BF16)
    packed = packed.reshape(depth, devices, cap, width).transpose(1, 0, 2, 3)
    packed = packed.reshape(devices * per_owner, width)
    arrived = lax.all_to_all(packed, ALL, 0, 0, tiled=True)
    arrived = arrived.reshape(leaves, depth, cores * per_owner, width).astype(F32).sum(1)
    arrived = arrived.reshape(leaves * cores * per_owner, width).astype(BF16)
    reduced = (rhs_parent.astype(F32) - matmul(place, arrived)).astype(BF16)

    fwd_parent = sum_leaves(matmul(inv_parent, gather_block(reduced)))
    sol_parent = scatter_block(matmul_t(inv_parent, fwd_parent))

    wanted = matmul_t(place, sol_parent).astype(BF16)
    wanted = wanted.reshape(leaves, 1, cores * per_owner, width)
    wanted = jnp.broadcast_to(wanted, (leaves, depth, cores * per_owner, width))
    got = lax.all_to_all(wanted.reshape(devices * per_owner, width), ALL, 0, 0, tiled=True)
    got = got.reshape(devices, depth, cap, width).transpose(1, 0, 2, 3)
    got = got.reshape(depth, devices * cap, width)
    picked = jnp.einsum("bsi,bsr->bir", pick, got, preferred_element_type=F32).astype(BF16)
    picked = picked.reshape(panel.shape[1], width)

    coupling = sum_cores(matmul_t(panel[0], picked))
    corrected = (forward.astype(F32) - coupling).astype(BF16)
    sol_leaf = sum_rows(matmul_t(inv_leaf[0], corrected).astype(BF16))
    return (sol_leaf[None], sol_parent)


def solution(mesh):
    in_specs = (
        P("leaf", "col", None),
        P(("leaf", "row", "col"), None),
        P("leaf", "row", "col"),
        P("leaf", "col", "row"),
        P("leaf", "col"),
        P(("row", "col"), "leaf"),
    )
    out_specs = (P("leaf", "col", None), P(("leaf", "row", "col"), None))
    return jax.shard_map(
        per_device, mesh=mesh, in_specs=in_specs, out_specs=out_specs, check_vma=False
    )
```

```python
import jax
import jax.experimental.pallas as pl
import jax.experimental.pallas.tpu as pltpu
import jax.numpy as jnp
from jax import lax
from jax.sharding import PartitionSpec as P

ALL = ("leaf", "row", "col")
F32 = jnp.float32
BF16 = jnp.bfloat16
CHUNKS = 12
VMEM = 56 * 2**20
DOTS = ((0, 2), (2, 2), (4, 4), (8, 4))


def matmul(a, x):
    return jnp.dot(a, x, preferred_element_type=F32)


def matmul_t(a, x):
    return lax.dot_general(a, x, (((0,), (0,)), ((), ())), preferred_element_type=F32)


def sum_cores(part):
    if lax.axis_size("col") == 2:
        other = lax.ppermute(part.astype(BF16), "col", [(0, 1), (1, 0)])
        return part + other.astype(F32)
    return lax.psum(part, "col")


def sum_leaves(part):
    size = lax.axis_size("leaf")
    bits = [1 << b for b in range(size.bit_length() - 1)]
    halves = jnp.split(part, 2, axis=0)
    orders = (bits, bits[::-1])
    for step in range(len(bits)):
        moved = [
            lax.ppermute(h.astype(BF16), "leaf", [(i, i ^ order[step]) for i in range(size)])
            for h, order in zip(halves, orders)
        ]
        halves = [h + m.astype(F32) for h, m in zip(halves, moved)]
    return jnp.concatenate(halves, axis=0).astype(BF16)


def gather_block(own):
    rows, cols = own.shape
    depth = lax.axis_size("row")
    z = lax.axis_index("row")
    parts = [own]
    for d in range(1, depth):
        parts.append(lax.ppermute(own, "row", [(i, (i + d) % depth) for i in range(depth)]))
    stacked = jnp.stack(parts)
    placed = jnp.take(stacked, (z - jnp.arange(depth)) % depth, axis=0, mode="clip")
    cores = lax.axis_size("col")
    if cores == 2:
        c = lax.axis_index("col")
        other = lax.ppermute(placed, "col", [(0, 1), (1, 0)])
        both = jnp.stack(
            [jnp.where(c == 0, placed, other), jnp.where(c == 0, other, placed)], axis=1
        )
    else:
        both = lax.all_gather(placed, "col", axis=1)
    return both.reshape(depth * cores * rows, cols)


def columns_t(a, x, core, depth, cores):
    k, m = a.shape
    rows = m // (depth * cores)
    z = lax.axis_index("row")
    which = jnp.stack([core, z]).astype(jnp.int32)

    def kernel(which_ref, a_ref, x_ref, out_ref):
        out_ref[0] = matmul_t(a_ref[...], x_ref[...]).astype(BF16)

    return pl.pallas_call(
        kernel,
        grid_spec=pltpu.PrefetchScalarGridSpec(
            num_scalar_prefetch=1,
            grid=(depth,),
            in_specs=[
                pl.BlockSpec(
                    (k, rows),
                    lambda d, which_ref: (0, lax.rem(which_ref[1] + d, depth) * cores + which_ref[0]),
                ),
                pl.BlockSpec((k, x.shape[1]), lambda d, which_ref: (0, 0)),
            ],
            out_specs=pl.BlockSpec((1, rows, x.shape[1]), lambda d, which_ref: (d, 0, 0)),
        ),
        out_shape=jax.ShapeDtypeStruct((depth, rows, x.shape[1]), BF16),
        compiler_params=pltpu.CompilerParams(vmem_limit_bytes=VMEM),
        cost_estimate=pl.CostEstimate(
            flops=2 * k * rows * depth * x.shape[1],
            bytes_accessed=2 * k * rows * depth,
            transcendentals=0,
        ),
    )(which, a, x)


def solve_and_scatter(a, x):
    depth = lax.axis_size("row")
    cores = lax.axis_size("col")
    if cores == 2:
        c = lax.axis_index("col")
        theirs = lax.ppermute(columns_t(a, x, 1 - c, depth, cores), "col", [(0, 1), (1, 0)])
        summed = columns_t(a, x, c, depth, cores) + theirs
    else:
        split = jnp.stack([columns_t(a, x, i, depth, cores) for i in range(cores)])
        summed = lax.psum_scatter(split.astype(F32), "col", scatter_dimension=0, tiled=True)
        summed = summed[0].astype(BF16)
    total = summed[0].astype(F32)
    for d in range(1, depth):
        moved = lax.ppermute(summed[d], "row", [(i, (i + d) % depth) for i in range(depth)])
        total = total + moved.astype(F32)
    return total.astype(BF16)


def solve_and_sum_rows(inverse, x):
    depth = lax.axis_size("row")
    if depth != 4:
        return lax.psum(matmul_t(inverse, x), "row").astype(BF16)
    width = inverse.shape[1]
    size = width // CHUNKS
    z = lax.axis_index("row")
    inner = (z == 1) | (z == 2)
    ends = [(0, 1), (1, 0), (2, 3), (3, 2)]
    middle = [(1, 2), (2, 1)]

    own = []
    for first, count in DOTS:
        cols = inverse[:, first * size : (first + count) * size]
        part = matmul_t(cols, x).astype(BF16)
        own.extend(jnp.split(part, count, axis=0))

    total = jnp.zeros((width, x.shape[1]), BF16)
    outer_got, middle_got = {}, {}
    for step in range(CHUNKS + 4):
        late = step - 4
        if late in middle_got and step < CHUNKS:
            send = jnp.where(inner, own[late] + middle_got[late], own[step])
        elif late in middle_got:
            send = own[late] + middle_got[late]
        else:
            send = own[step]
        mid = step - 2
        if 0 <= mid < CHUNKS:
            both = own[mid] + outer_got[mid]
            send, both, outer_got[mid] = lax.optimization_barrier((send, both, outer_got[mid]))
            outer_got[step] = lax.ppermute(send, "row", ends)
            middle_got[mid] = lax.ppermute(both, "row", middle)
        else:
            outer_got[step] = lax.ppermute(send, "row", ends)
        if late >= 0:
            others = jnp.where(
                inner,
                outer_got[late].astype(F32) + middle_got[late].astype(F32),
                outer_got[step].astype(F32),
            )
            done = (own[late].astype(F32) + others).astype(BF16)
            total = lax.dynamic_update_slice_in_dim(total, done, late * size, 0)
    return total


def slots_of(row_map, own, devices, depth):
    blocks = row_map.reshape(depth, -1)
    size = blocks.shape[1]
    cap = -(-size // devices)
    owner = blocks // own
    earlier = jnp.arange(size)[None, :] < jnp.arange(size)[:, None]
    rank = jnp.sum((owner[:, :, None] == owner[:, None, :]) & earlier[None], axis=2, dtype=jnp.int32)
    slot = owner * cap + rank
    hit = slot[:, None, :] == jnp.arange(devices * cap, dtype=jnp.int32)[None, :, None]
    local = jnp.max(jnp.where(hit, (blocks % own)[:, None, :], -1), axis=2)
    local = local.reshape(depth, devices, cap).transpose(1, 0, 2).reshape(devices, depth * cap)
    return hit.astype(BF16), local


def per_device(rhs_leaf, rhs_parent, inv_leaf, panel, row_map, inv_parent):
    leaves, depth, cores = (lax.axis_size(a) for a in ALL)
    devices = leaves * depth * cores
    me = lax.axis_index(ALL)
    own, width = rhs_parent.shape

    pick, local = slots_of(row_map[0], own, devices, depth)
    per_owner = local.shape[1]
    cap = per_owner // depth
    lists = lax.all_gather(local, ("leaf", "col"))
    mine = lax.dynamic_index_in_dim(lists, me, 1, keepdims=False).reshape(-1)
    place = (mine[None, :] == jnp.arange(own, dtype=jnp.int32)[:, None]).astype(BF16)

    forward = sum_cores(matmul(inv_leaf[0], rhs_leaf[0])).astype(BF16)
    update = matmul(panel[0], forward).astype(BF16).reshape(depth, -1, width)
    packed = jnp.einsum("bsi,bir->bsr", pick, update, preferred_element_type=F32).astype(BF16)
    packed = packed.reshape(depth, devices, cap, width).transpose(1, 0, 2, 3)
    packed = packed.reshape(devices * per_owner, width)
    arrived = lax.all_to_all(packed, ALL, 0, 0, tiled=True)
    arrived = arrived.reshape(leaves, depth, cores * per_owner, width).astype(F32).sum(1)
    arrived = arrived.reshape(leaves * cores * per_owner, width).astype(BF16)
    reduced = (rhs_parent.astype(F32) - matmul(place, arrived)).astype(BF16)

    fwd_parent = sum_leaves(matmul(inv_parent, gather_block(reduced)))
    sol_parent = solve_and_scatter(inv_parent, fwd_parent)

    wanted = matmul_t(place, sol_parent).astype(BF16)
    wanted = wanted.reshape(leaves, 1, cores * per_owner, width)
    wanted = jnp.broadcast_to(wanted, (leaves, depth, cores * per_owner, width))
    got = lax.all_to_all(wanted.reshape(devices * per_owner, width), ALL, 0, 0, tiled=True)
    got = got.reshape(devices, depth, cap, width).transpose(1, 0, 2, 3)
    got = got.reshape(depth, devices * cap, width)
    picked = jnp.einsum("bsi,bsr->bir", pick, got, preferred_element_type=F32).astype(BF16)
    picked = picked.reshape(panel.shape[1], width)

    coupling = sum_cores(matmul_t(panel[0], picked))
    corrected = (forward.astype(F32) - coupling).astype(BF16)
    sol_leaf = solve_and_sum_rows(inv_leaf[0], corrected)
    return (sol_leaf[None], sol_parent)


def solution(mesh):
    in_specs = (
        P("leaf", "col", None),
        P(("leaf", "row", "col"), None),
        P("leaf", "row", "col"),
        P("leaf", "col", "row"),
        P("leaf", "col"),
        P(("row", "col"), "leaf"),
    )
    out_specs = (P("leaf", "col", None), P(("leaf", "row", "col"), None))
    return jax.shard_map(
        per_device, mesh=mesh, in_specs=in_specs, out_specs=out_specs, check_vma=False
    )
```

```python
import jax
import jax.experimental.pallas as pl
import jax.experimental.pallas.tpu as pltpu
import jax.numpy as jnp
from jax import lax
from jax.sharding import PartitionSpec as P

ALL = ("leaf", "row", "col")
F32 = jnp.float32
BF16 = jnp.bfloat16
CHUNKS = 12
GROUP = 2
VMEM = 40 * 2**20


def matmul(a, x):
    return jnp.dot(a, x, preferred_element_type=F32)


def matmul_t(a, x):
    return lax.dot_general(a, x, (((0,), (0,)), ((), ())), preferred_element_type=F32)


def sum_cores(part):
    if lax.axis_size("col") == 2:
        other = lax.ppermute(part.astype(BF16), "col", [(0, 1), (1, 0)])
        return part + other.astype(F32)
    return lax.psum(part, "col")


def swap_leaves(halves, steps):
    size = lax.axis_size("leaf")
    bits = [1 << b for b in range(size.bit_length() - 1)]
    orders = (bits, bits[::-1])
    for step in range(len(bits))[steps]:
        moved = [
            lax.ppermute(h.astype(BF16), "leaf", [(i, i ^ order[step]) for i in range(size)])
            for h, order in zip(halves, orders)
        ]
        halves = [h + m.astype(F32) for h, m in zip(halves, moved)]
    return halves


def gather_lists(local):
    size = lax.axis_size("leaf")
    parts = [local] + [
        lax.ppermute(local, "leaf", [(i, i ^ d) for i in range(size)]) for d in range(1, size)
    ]
    order = lax.axis_index("leaf") ^ jnp.arange(size)
    lists = jnp.take(jnp.stack(parts), order, axis=0, mode="clip")
    if lax.axis_size("col") == 2:
        c = lax.axis_index("col")
        other = lax.ppermute(lists, "col", [(0, 1), (1, 0)])
        return jnp.stack([jnp.where(c == 0, lists, other), jnp.where(c == 0, other, lists)], axis=1)
    return lax.all_gather(lists, "col", axis=1)


def gather_block(own):
    depth = lax.axis_size("row")
    z = lax.axis_index("row")
    parts = [own] + [
        lax.ppermute(own, "row", [(i, (i + d) % depth) for i in range(depth)])
        for d in range(1, depth)
    ]
    cores = lax.axis_size("col")
    if cores == 2:
        c = lax.axis_index("col")
        parts += [lax.ppermute(part, "col", [(0, 1), (1, 0)]) for part in parts]
        place = jnp.arange(depth * cores)
        source = (z - place // cores) % depth + depth * ((place % cores) ^ c)
    else:
        parts = [lax.all_gather(jnp.stack(parts), "col", axis=1)]
        place = jnp.arange(depth * cores)
        source = (z - place // cores) % depth * cores + place % cores
    parts = jnp.stack(parts).reshape(depth * cores, *own.shape)
    return jnp.take(parts, source, axis=0, mode="clip").reshape(-1, own.shape[1])


def columns_t(a, x, depth, cores):
    k, m = a.shape
    rows = m // (depth * cores)
    width = x.shape[1]
    which = jnp.stack([lax.axis_index("col"), lax.axis_index("row")]).astype(jnp.int32)

    def kernel(which_ref, a_ref, x_ref, out_ref):
        for e in range(cores):
            core = lax.rem(which_ref[0] + 1 + e, cores)
            cols = pl.ds(pl.multiple_of(core * rows, rows), rows)
            out_ref[e, 0] = matmul_t(a_ref[:, cols], x_ref[...]).astype(BF16)

    return pl.pallas_call(
        kernel,
        grid_spec=pltpu.PrefetchScalarGridSpec(
            num_scalar_prefetch=1,
            grid=(depth,),
            in_specs=[
                pl.BlockSpec(
                    (k, cores * rows),
                    lambda d, which_ref: (0, lax.rem(which_ref[1] + d, depth)),
                ),
                pl.BlockSpec((k, width), lambda d, which_ref: (0, 0)),
            ],
            out_specs=pl.BlockSpec((cores, 1, rows, width), lambda d, which_ref: (0, d, 0, 0)),
        ),
        out_shape=jax.ShapeDtypeStruct((cores, depth, rows, width), BF16),
        compiler_params=pltpu.CompilerParams(vmem_limit_bytes=VMEM),
        cost_estimate=pl.CostEstimate(
            flops=2 * k * m * width, bytes_accessed=2 * k * m, transcendentals=0
        ),
    )(which, a, x)


def dot_t(a, x, first, count, tile, dtype):
    k = a.shape[0]
    width = x.shape[1]

    def kernel(a_ref, x_ref, *out_refs):
        part = matmul_t(a_ref[...], x_ref[...]).astype(dtype)
        for j, out_ref in enumerate(out_refs):

            @pl.when(pl.program_id(0) == j)
            def _():
                out_ref[...] = part

    return pl.pallas_call(
        kernel,
        grid=(count,),
        in_specs=[
            pl.BlockSpec((k, tile), lambda i: (0, first + i)),
            pl.BlockSpec((k, width), lambda i: (0, 0)),
        ],
        out_specs=[pl.BlockSpec((tile, width), lambda i: (0, 0))] * count,
        out_shape=[jax.ShapeDtypeStruct((tile, width), dtype)] * count,
        compiler_params=pltpu.CompilerParams(vmem_limit_bytes=VMEM),
        cost_estimate=pl.CostEstimate(
            flops=2 * k * count * tile * width,
            bytes_accessed=2 * k * count * tile,
            transcendentals=0,
        ),
    )(a, x)


def matmul_t_tiled(a, x):
    k, m = a.shape
    width = x.shape[1]
    tile = min(m, 1024)

    def kernel(a_ref, x_ref, out_ref):
        out_ref[...] = matmul_t(a_ref[...], x_ref[...])

    return pl.pallas_call(
        kernel,
        grid=(m // tile,),
        in_specs=[
            pl.BlockSpec((k, tile), lambda i: (0, i)),
            pl.BlockSpec((k, width), lambda i: (0, 0)),
        ],
        out_specs=pl.BlockSpec((tile, width), lambda i: (i, 0)),
        out_shape=jax.ShapeDtypeStruct((m, width), F32),
        compiler_params=pltpu.CompilerParams(vmem_limit_bytes=VMEM),
        cost_estimate=pl.CostEstimate(
            flops=2 * k * m * width, bytes_accessed=2 * k * m, transcendentals=0
        ),
    )(a, x)


def solve_and_swap(a, x):
    cores = lax.axis_size("col")
    parts = columns_t(a, x, lax.axis_size("row"), cores)
    total = parts[-1]
    for e in range(cores - 1):
        total = total + lax.ppermute(
            parts[e], "col", [(i, (i + 1 + e) % cores) for i in range(cores)]
        )
    return total


def scatter_rows(summed):
    depth = lax.axis_size("row")
    total = summed[0].astype(F32)
    for d in range(1, depth):
        moved = lax.ppermute(summed[d], "row", [(i, (i + d) % depth) for i in range(depth)])
        total = total + moved.astype(F32)
    return total.astype(BF16)


def solve_and_sum_rows(inverse, x):
    depth = lax.axis_size("row")
    if depth != 4:
        return lax.psum(matmul_t(inverse, x), "row").astype(BF16)
    width = inverse.shape[1]
    size = width // CHUNKS
    z = lax.axis_index("row")
    inner = (z == 1) | (z == 2)
    ends = [(0, 1), (1, 0), (2, 3), (3, 2)]
    middle = [(1, 2), (2, 1)]

    def group(first, x):
        return dot_t(inverse, x, first, GROUP, size, BF16)

    total = jnp.zeros((width, x.shape[1]), BF16)
    own, outer_got, middle_got = list(group(0, x)), [], []
    for step in range(CHUNKS + 4):
        late = step - 4
        if late >= 0 and step < CHUNKS:
            send = jnp.where(inner, own[late] + middle_got[late], own[step])
        elif late >= 0:
            send = own[late] + middle_got[late]
        else:
            send = own[step]
        mid = step - 2
        if 0 <= mid < CHUNKS:
            both = own[mid] + outer_got[mid]
            send, both, outer_got[mid] = lax.optimization_barrier((send, both, outer_got[mid]))
            middle_got.append(lax.ppermute(both, "row", middle))
        if len(own) < CHUNKS and step >= len(own) - 1:
            x, send = lax.optimization_barrier((x, send))
            own.extend(group(len(own), x))
        outer_got.append(lax.ppermute(send, "row", ends))
        if late >= 0:
            others = jnp.where(
                inner,
                outer_got[late].astype(F32) + middle_got[late].astype(F32),
                outer_got[step].astype(F32),
            )
            done = (own[late].astype(F32) + others).astype(BF16)
            total = lax.dynamic_update_slice_in_dim(total, done, late * size, 0)
    return total


def slots_of(row_map, own, devices, depth):
    blocks = row_map.reshape(depth, -1)
    size = blocks.shape[1]
    cap = -(-size // devices)
    owner = blocks // own
    earlier = jnp.arange(size)[None, :] < jnp.arange(size)[:, None]
    rank = jnp.sum((owner[:, :, None] == owner[:, None, :]) & earlier[None], axis=2, dtype=jnp.int32)
    slot = owner * cap + rank
    hit = slot[:, None, :] == jnp.arange(devices * cap, dtype=jnp.int32)[None, :, None]
    local = jnp.max(jnp.where(hit, (blocks % own)[:, None, :], -1), axis=2)
    local = local.reshape(depth, devices, cap).transpose(1, 0, 2).reshape(devices, depth * cap)
    return hit.astype(BF16), local


def per_device(rhs_leaf, rhs_parent, inv_leaf, panel, row_map, inv_parent):
    leaves, depth, cores = (lax.axis_size(a) for a in ALL)
    devices = leaves * depth * cores
    me = lax.axis_index(ALL)
    own, width = rhs_parent.shape

    pick, local = slots_of(row_map[0], own, devices, depth)
    per_owner = local.shape[1]
    cap = per_owner // depth
    lists = gather_lists(local)
    mine = lax.dynamic_index_in_dim(lists, me, 2, keepdims=False).reshape(-1)
    place = (mine[None, :] == jnp.arange(own, dtype=jnp.int32)[:, None]).astype(BF16)

    forward = sum_cores(matmul(inv_leaf[0], rhs_leaf[0])).astype(BF16)
    update = matmul(panel[0], forward).astype(BF16).reshape(depth, -1, width)
    packed = jnp.einsum("bsi,bir->bsr", pick, update, preferred_element_type=F32).astype(BF16)
    packed = packed.reshape(depth, devices, cap, width).transpose(1, 0, 2, 3)
    packed = packed.reshape(devices * per_owner, width)

    arrived = lax.all_to_all(packed, ALL, 0, 0, tiled=True)
    arrived = arrived.reshape(leaves, depth, cores * per_owner, width).astype(F32).sum(1)
    arrived = arrived.reshape(leaves * cores * per_owner, width).astype(BF16)
    reduced = (rhs_parent.astype(F32) - matmul(place, arrived)).astype(BF16)

    whole = gather_block(reduced)
    halves = swap_leaves(jnp.split(matmul(inv_parent, whole), 2, axis=0), slice(0, None))
    fwd_parent = jnp.concatenate(halves, axis=0).astype(BF16)
    sol_parent = scatter_rows(solve_and_swap(inv_parent, fwd_parent))

    wanted = matmul_t(place, sol_parent).astype(BF16)
    wanted = wanted.reshape(leaves, 1, cores * per_owner, width)
    wanted = jnp.broadcast_to(wanted, (leaves, depth, cores * per_owner, width))
    got = lax.all_to_all(wanted.reshape(devices * per_owner, width), ALL, 0, 0, tiled=True)
    got = got.reshape(devices, depth, cap, width).transpose(1, 0, 2, 3)
    got = got.reshape(depth, devices * cap, width)
    picked = jnp.einsum("bsi,bsr->bir", pick, got, preferred_element_type=F32).astype(BF16)
    picked = picked.reshape(panel.shape[1], width)

    coupling = sum_cores(matmul_t_tiled(panel[0], picked))
    corrected = (forward.astype(F32) - coupling).astype(BF16)
    sol_leaf = solve_and_sum_rows(inv_leaf[0], corrected)
    return (sol_leaf[None], sol_parent)


def solution(mesh):
    in_specs = (
        P("leaf", "col", None),
        P(("leaf", "row", "col"), None),
        P("leaf", "row", "col"),
        P("leaf", "col", "row"),
        P("leaf", "col"),
        P(("row", "col"), "leaf"),
    )
    out_specs = (P("leaf", "col", None), P(("leaf", "row", "col"), None))
    return jax.shard_map(
        per_device, mesh=mesh, in_specs=in_specs, out_specs=out_specs, check_vma=False
    )
```

```python
import jax
import jax.experimental.pallas as pl
import jax.experimental.pallas.tpu as pltpu
import jax.numpy as jnp
from jax import lax
from jax.sharding import PartitionSpec as P

ALL = ("leaf", "row", "col")
F32 = jnp.float32
BF16 = jnp.bfloat16
CHUNKS = 12
GROUPS = (1, 1, 2, 2, 2, 2, 2)
VMEM = 40 * 2**20
RESIDENT = 8 * 2**20


def matmul(a, x):
    return jnp.dot(a, x, preferred_element_type=F32)


def matmul_t(a, x):
    return lax.dot_general(a, x, (((0,), (0,)), ((), ())), preferred_element_type=F32)


def sum_cores(part):
    if lax.axis_size("col") == 2:
        other = lax.ppermute(part, "col", [(0, 1), (1, 0)])
        return part.astype(F32) + other.astype(F32)
    return lax.psum(part.astype(F32), "col")


def swap_leaves(halves, steps):
    size = lax.axis_size("leaf")
    bits = [1 << b for b in range(size.bit_length() - 1)]
    orders = (bits, bits[::-1])
    for step in range(len(bits))[steps]:
        moved = [
            lax.ppermute(h.astype(BF16), "leaf", [(i, i ^ order[step]) for i in range(size)])
            for h, order in zip(halves, orders)
        ]
        halves = [h + m.astype(F32) for h, m in zip(halves, moved)]
    return halves


def gather_lists(local):
    size = lax.axis_size("leaf")
    parts = [local] + [
        lax.ppermute(local, "leaf", [(i, i ^ d) for i in range(size)]) for d in range(1, size)
    ]
    order = lax.axis_index("leaf") ^ jnp.arange(size)
    lists = jnp.take(jnp.stack(parts), order, axis=0, mode="clip")
    if lax.axis_size("col") == 2:
        c = lax.axis_index("col")
        other = lax.ppermute(lists, "col", [(0, 1), (1, 0)])
        return jnp.stack([jnp.where(c == 0, lists, other), jnp.where(c == 0, other, lists)], axis=1)
    return lax.all_gather(lists, "col", axis=1)


def matmul_streamed(a, x, dtype):
    m, k = a.shape
    width = x.shape[1]
    tile = m // 6 if m % 96 == 0 else m
    count = m // tile
    slots = min(3, count)

    x = pltpu.with_memory_space_constraint(x, pltpu.HBM)

    def kernel(a_ref, x_ref, out_ref, held, x_held, sems, x_sem):
        def copy(t, slot):
            rows = pl.ds(pl.multiple_of(t * tile, tile), tile)
            return pltpu.make_async_copy(a_ref.at[rows, :], held.at[slot], sems.at[slot])

        x_copy = pltpu.make_async_copy(x_ref, x_held, x_sem)
        x_copy.start()
        for t in range(slots):
            copy(t, t).start()
        x_copy.wait()

        @pl.loop(0, count)
        def _(t):
            slot = lax.rem(t, slots)
            copy(t, slot).wait()
            rows = pl.ds(pl.multiple_of(t * tile, tile), tile)
            out_ref[rows, :] = matmul(held[slot], x_held[...]).astype(dtype)

            @pl.when(t + slots < count)
            def _():
                copy(t + slots, slot).start()

    return pl.pallas_call(
        kernel,
        in_specs=[pl.BlockSpec(memory_space=pltpu.HBM)] * 2,
        out_specs=pl.BlockSpec(memory_space=pltpu.VMEM),
        out_shape=jax.ShapeDtypeStruct((m, width), dtype),
        scratch_shapes=[
            pltpu.VMEM((slots, tile, k), BF16),
            pltpu.VMEM((k, width), BF16),
            pltpu.SemaphoreType.DMA((slots,)),
            pltpu.SemaphoreType.DMA,
        ],
        compiler_params=pltpu.CompilerParams(vmem_limit_bytes=VMEM),
        cost_estimate=pl.CostEstimate(
            flops=2 * m * k * width, bytes_accessed=2 * m * k, transcendentals=0
        ),
    )(a, x)


def add_columns(a, parts, chunks, total):
    m, k = a.shape
    rows, width = parts[0].shape
    count = len(parts)
    tile = min(m, 512)

    def kernel(chunks_ref, a_ref, *refs):
        out_ref = refs[-1]

        @pl.loop(0, m // tile)
        def _(i):
            at = pl.ds(pl.multiple_of(i * tile, tile), tile)
            acc = jnp.zeros((tile, width), F32) if total is None else refs[count][at, :]
            for j in range(count):
                cols = pl.ds(pl.multiple_of(chunks_ref[j] * rows, rows), rows)
                acc = acc + matmul(a_ref[at, cols], refs[j][...])
            out_ref[at, :] = acc

    extra = [] if total is None else [total]
    return pl.pallas_call(
        kernel,
        in_specs=[pl.BlockSpec(memory_space=pltpu.SMEM)]
        + [pl.BlockSpec(memory_space=pltpu.VMEM)] * (1 + count + len(extra)),
        out_specs=pl.BlockSpec(memory_space=pltpu.VMEM),
        out_shape=jax.ShapeDtypeStruct((m, width), F32),
        compiler_params=pltpu.CompilerParams(vmem_limit_bytes=RESIDENT),
        cost_estimate=pl.CostEstimate(
            flops=2 * m * rows * count * width, bytes_accessed=0, transcendentals=0
        ),
    )(jnp.stack(chunks).astype(jnp.int32), a, *parts, *extra)


def first_columns(a, parts, chunks):
    m, k = a.shape
    rows, width = parts[0].shape
    count = len(parts)

    def kernel(chunks_ref, a_ref, *refs):
        out_ref = refs[-1]
        for j in range(count):

            @pl.when(pl.program_id(0) == j)
            def _():
                part = matmul(a_ref[...], refs[j][...])
                out_ref[...] = part if j == 0 else part + out_ref[...]

    return pl.pallas_call(
        kernel,
        grid_spec=pltpu.PrefetchScalarGridSpec(
            num_scalar_prefetch=1,
            grid=(count,),
            in_specs=[pl.BlockSpec((m, rows), lambda i, chunks_ref: (0, chunks_ref[i]))]
            + [pl.BlockSpec((rows, width), lambda i, chunks_ref: (0, 0))] * count,
            out_specs=pl.BlockSpec((m, width), lambda i, chunks_ref: (0, 0)),
        ),
        out_shape=jax.ShapeDtypeStruct((m, width), F32),
        compiler_params=pltpu.CompilerParams(vmem_limit_bytes=VMEM),
        cost_estimate=pl.CostEstimate(
            flops=2 * m * rows * count * width,
            bytes_accessed=4 * m * rows * count,
            transcendentals=0,
        ),
    )(jnp.stack(chunks).astype(jnp.int32), a, *parts)


def gather_and_solve(a, own):
    depth = lax.axis_size("row")
    cores = lax.axis_size("col")
    z = lax.axis_index("row")
    c = lax.axis_index("col")
    rows = [own] + [
        lax.ppermute(own, "row", [(i, (i + d) % depth) for i in range(depth)])
        for d in range(1, depth)
    ]
    total = None
    step = max(depth // 2, 1)
    for first in range(0, depth, step):
        parts, chunks = [], []
        if total is not None:
            rows[first:], total = lax.optimization_barrier((rows[first:], total))
        for d in range(first, min(first + step, depth)):
            for e in range(cores):
                part = rows[d]
                if e > 0:
                    part = lax.ppermute(part, "col", [(i, (i + e) % cores) for i in range(cores)])
                parts.append(part)
                chunks.append((z - d) % depth * cores + (c - e) % cores)
        if total is None:
            total = first_columns(a, parts, chunks)
        else:
            total = add_columns(a, parts, chunks, total)
    return total


def columns_t(a, x, depth, cores):
    k, m = a.shape
    rows = m // (depth * cores)
    width = x.shape[1]
    which = jnp.stack([lax.axis_index("col"), lax.axis_index("row")]).astype(jnp.int32)

    def kernel(which_ref, a_ref, x_ref, out_ref):
        @pl.loop(0, cores * depth)
        def _(i):
            core = lax.rem(which_ref[0] + 1 + lax.div(i, depth), cores)
            z = lax.rem(which_ref[1] + i, depth)
            cols = pl.ds(pl.multiple_of((z * cores + core) * rows, rows), rows)
            out_ref[i] = matmul_t(a_ref[:, cols], x_ref[...]).astype(BF16)

    out = pl.pallas_call(
        kernel,
        in_specs=[pl.BlockSpec(memory_space=pltpu.SMEM)]
        + [pl.BlockSpec(memory_space=pltpu.VMEM)] * 2,
        out_specs=pl.BlockSpec(memory_space=pltpu.VMEM),
        out_shape=jax.ShapeDtypeStruct((cores * depth, rows, width), BF16),
        compiler_params=pltpu.CompilerParams(vmem_limit_bytes=RESIDENT),
        cost_estimate=pl.CostEstimate(
            flops=2 * k * m * width, bytes_accessed=0, transcendentals=0
        ),
    )(which, a, x)
    return out.reshape(cores, depth, rows, width)


def dot_t(a, x, first, count, tile, dtype):
    k = a.shape[0]
    width = x.shape[1]

    def kernel(a_ref, x_ref, *out_refs):
        part = matmul_t(a_ref[...], x_ref[...]).astype(dtype)
        for j, out_ref in enumerate(out_refs):

            @pl.when(pl.program_id(0) == j)
            def _():
                out_ref[...] = part

    return pl.pallas_call(
        kernel,
        grid=(count,),
        in_specs=[
            pl.BlockSpec((k, tile), lambda i: (0, first + i)),
            pl.BlockSpec((k, width), lambda i: (0, 0)),
        ],
        out_specs=[pl.BlockSpec((tile, width), lambda i: (0, 0))] * count,
        out_shape=[jax.ShapeDtypeStruct((tile, width), dtype)] * count,
        compiler_params=pltpu.CompilerParams(vmem_limit_bytes=VMEM),
        cost_estimate=pl.CostEstimate(
            flops=2 * k * count * tile * width,
            bytes_accessed=2 * k * count * tile,
            transcendentals=0,
        ),
    )(a, x)


def matmul_t_tiled(a, x):
    k, m = a.shape
    width = x.shape[1]
    tile = min(m, 1024)

    def kernel(a_ref, x_ref, out_ref):
        out_ref[...] = matmul_t(a_ref[...], x_ref[...]).astype(BF16)

    return pl.pallas_call(
        kernel,
        grid=(m // tile,),
        in_specs=[
            pl.BlockSpec((k, tile), lambda i: (0, i)),
            pl.BlockSpec((k, width), lambda i: (0, 0)),
        ],
        out_specs=pl.BlockSpec((tile, width), lambda i: (i, 0)),
        out_shape=jax.ShapeDtypeStruct((m, width), BF16),
        compiler_params=pltpu.CompilerParams(vmem_limit_bytes=VMEM),
        cost_estimate=pl.CostEstimate(
            flops=2 * k * m * width, bytes_accessed=2 * k * m, transcendentals=0
        ),
    )(a, x)


def solve_and_scatter(a, x):
    depth = lax.axis_size("row")
    cores = lax.axis_size("col")
    parts = columns_t(a, x, depth, cores)
    summed = parts[-1]
    for e in range(cores - 1):
        summed = summed + lax.ppermute(
            parts[e], "col", [(i, (i + 1 + e) % cores) for i in range(cores)]
        )
    total = summed[0].astype(F32)
    for d in range(1, depth):
        moved = lax.ppermute(summed[d], "row", [(j, (j + d) % depth) for j in range(depth)])
        total = total + moved.astype(F32)
    return total.astype(BF16)


def solve_and_sum_rows(inverse, x):
    depth = lax.axis_size("row")
    if depth != 4:
        return lax.psum(matmul_t(inverse, x), "row").astype(BF16)
    width = inverse.shape[1]
    size = width // CHUNKS
    z = lax.axis_index("row")
    inner = (z == 1) | (z == 2)
    ends = [(0, 1), (1, 0), (2, 3), (3, 2)]
    middle = [(1, 2), (2, 1)]

    def group(first, x):
        return dot_t(inverse, x, first, sizes.pop(0), size, BF16)

    total = jnp.zeros((width, x.shape[1]), BF16)
    sizes = list(GROUPS)
    own, outer_got, middle_got = list(group(0, x)), [], []
    for step in range(CHUNKS + 4):
        late = step - 4
        if late >= 0 and step < CHUNKS:
            send = jnp.where(inner, own[late] + middle_got[late], own[step])
        elif late >= 0:
            send = own[late] + middle_got[late]
        else:
            send = own[step]
        mid = step - 2
        if 0 <= mid < CHUNKS:
            both = own[mid] + outer_got[mid]
            send, both, outer_got[mid] = lax.optimization_barrier((send, both, outer_got[mid]))
            middle_got.append(lax.ppermute(both, "row", middle))
        if len(own) < CHUNKS and step >= len(own) - 1:
            x, send = lax.optimization_barrier((x, send))
            own.extend(group(len(own), x))
        outer_got.append(lax.ppermute(send, "row", ends))
        if late >= 0:
            others = jnp.where(
                inner,
                outer_got[late].astype(F32) + middle_got[late].astype(F32),
                outer_got[step].astype(F32),
            )
            done = (own[late].astype(F32) + others).astype(BF16)
            total = lax.dynamic_update_slice_in_dim(total, done, late * size, 0)
    return total


def slots_of(row_map, own, devices, depth):
    blocks = row_map.reshape(depth, -1)
    size = blocks.shape[1]
    cap = -(-size // devices)
    owner = blocks // own
    earlier = jnp.arange(size)[None, :] < jnp.arange(size)[:, None]
    rank = jnp.sum((owner[:, :, None] == owner[:, None, :]) & earlier[None], axis=2, dtype=jnp.int32)
    slot = owner * cap + rank
    hit = slot[:, None, :] == jnp.arange(devices * cap, dtype=jnp.int32)[None, :, None]
    local = jnp.max(jnp.where(hit, (blocks % own)[:, None, :], -1), axis=2)
    local = local.reshape(depth, devices, cap).transpose(1, 0, 2).reshape(devices, depth * cap)
    return hit.astype(BF16), local


def per_device(rhs_leaf, rhs_parent, inv_leaf, panel, row_map, inv_parent):
    leaves, depth, cores = (lax.axis_size(a) for a in ALL)
    devices = leaves * depth * cores
    me = lax.axis_index(ALL)
    own, width = rhs_parent.shape

    pick, local = slots_of(row_map[0], own, devices, depth)
    per_owner = local.shape[1]
    cap = per_owner // depth
    lists = gather_lists(local)
    mine = lax.dynamic_index_in_dim(lists, me, 2, keepdims=False).reshape(-1)
    place = (mine[None, :] == jnp.arange(own, dtype=jnp.int32)[:, None]).astype(BF16)

    forward = sum_cores(matmul_streamed(inv_leaf[0], rhs_leaf[0], BF16)).astype(BF16)
    update = matmul_streamed(panel[0], forward, BF16).reshape(depth, -1, width)
    packed = jnp.einsum("bsi,bir->bsr", pick, update, preferred_element_type=F32).astype(BF16)
    packed = packed.reshape(depth, devices, cap, width).transpose(1, 0, 2, 3)
    packed = packed.reshape(devices * per_owner, width)

    arrived = lax.all_to_all(packed, ALL, 0, 0, tiled=True)
    arrived = arrived.reshape(leaves, depth, cores * per_owner, width).astype(F32).sum(1)
    arrived = arrived.reshape(leaves * cores * per_owner, width).astype(BF16)
    reduced = (rhs_parent.astype(F32) - matmul(place, arrived)).astype(BF16)

    part = gather_and_solve(inv_parent, reduced)
    halves = swap_leaves(jnp.split(part, 2, axis=0), slice(0, None))
    fwd_parent = jnp.concatenate(halves, axis=0).astype(BF16)
    sol_parent = solve_and_scatter(inv_parent, fwd_parent)

    wanted = matmul_t(place, sol_parent).astype(BF16)
    wanted = wanted.reshape(leaves, 1, cores * per_owner, width)
    wanted = jnp.broadcast_to(wanted, (leaves, depth, cores * per_owner, width))
    got = lax.all_to_all(wanted.reshape(devices * per_owner, width), ALL, 0, 0, tiled=True)
    got = got.reshape(devices, depth, cap, width).transpose(1, 0, 2, 3)
    got = got.reshape(depth, devices * cap, width)
    picked = jnp.einsum("bsi,bsr->bir", pick, got, preferred_element_type=F32).astype(BF16)
    picked = picked.reshape(panel.shape[1], width)

    coupling = sum_cores(matmul_t_tiled(panel[0], picked))
    corrected = (forward.astype(F32) - coupling).astype(BF16)
    sol_leaf = solve_and_sum_rows(inv_leaf[0], corrected)
    return (sol_leaf[None], sol_parent)


def solution(mesh):
    in_specs = (
        P("leaf", "col", None),
        P(("leaf", "row", "col"), None),
        P("leaf", "row", "col"),
        P("leaf", "col", "row"),
        P("leaf", "col"),
        P(("row", "col"), "leaf"),
    )
    out_specs = (P("leaf", "col", None), P(("leaf", "row", "col"), None))
    return jax.shard_map(
        per_device, mesh=mesh, in_specs=in_specs, out_specs=out_specs, check_vma=False
    )
```

```python
import jax
import jax.experimental.pallas as pl
import jax.experimental.pallas.tpu as pltpu
import jax.numpy as jnp
from jax import lax
from jax.sharding import PartitionSpec as P

ALL = ("leaf", "row", "col")
F32 = jnp.float32
BF16 = jnp.bfloat16
CHUNKS = 12
GROUPS = (1, 1, 2, 2, 2, 2, 2)
VMEM = 40 * 2**20
RESIDENT = 8 * 2**20


def matmul(a, x):
    return jnp.dot(a, x, preferred_element_type=F32)


def matmul_t(a, x):
    return lax.dot_general(a, x, (((0,), (0,)), ((), ())), preferred_element_type=F32)


def sum_cores(part):
    if lax.axis_size("col") == 2:
        other = lax.ppermute(part, "col", [(0, 1), (1, 0)])
        return part.astype(F32) + other.astype(F32)
    return lax.psum(part.astype(F32), "col")


def swap_leaves(halves, steps):
    size = lax.axis_size("leaf")
    bits = [1 << b for b in range(size.bit_length() - 1)]
    orders = (bits, bits[::-1])
    for step in range(len(bits))[steps]:
        moved = [
            lax.ppermute(h.astype(BF16), "leaf", [(i, i ^ order[step]) for i in range(size)])
            for h, order in zip(halves, orders)
        ]
        halves = [h + m.astype(F32) for h, m in zip(halves, moved)]
    return halves


def gather_lists(local):
    size = lax.axis_size("leaf")
    parts = [local] + [
        lax.ppermute(local, "leaf", [(i, i ^ d) for i in range(size)]) for d in range(1, size)
    ]
    order = lax.axis_index("leaf") ^ jnp.arange(size)
    lists = jnp.take(jnp.stack(parts), order, axis=0, mode="clip")
    if lax.axis_size("col") == 2:
        c = lax.axis_index("col")
        other = lax.ppermute(lists, "col", [(0, 1), (1, 0)])
        return jnp.stack([jnp.where(c == 0, lists, other), jnp.where(c == 0, other, lists)], axis=1)
    return lax.all_gather(lists, "col", axis=1)


def matmul_streamed(a, x, dtype):
    m, k = a.shape
    width = x.shape[1]
    tile = m // 6 if m % 96 == 0 else m
    count = m // tile
    slots = min(3, count)

    x = pltpu.with_memory_space_constraint(x, pltpu.HBM)

    def kernel(a_ref, x_ref, out_ref, held, x_held, sems, x_sem):
        def copy(t, slot):
            rows = pl.ds(pl.multiple_of(t * tile, tile), tile)
            return pltpu.make_async_copy(a_ref.at[rows, :], held.at[slot], sems.at[slot])

        x_copy = pltpu.make_async_copy(x_ref, x_held, x_sem)
        x_copy.start()
        for t in range(slots):
            copy(t, t).start()
        x_copy.wait()

        @pl.loop(0, count)
        def _(t):
            slot = lax.rem(t, slots)
            copy(t, slot).wait()
            rows = pl.ds(pl.multiple_of(t * tile, tile), tile)
            out_ref[rows, :] = matmul(held[slot], x_held[...]).astype(dtype)

            @pl.when(t + slots < count)
            def _():
                copy(t + slots, slot).start()

    return pl.pallas_call(
        kernel,
        in_specs=[pl.BlockSpec(memory_space=pltpu.HBM)] * 2,
        out_specs=pl.BlockSpec(memory_space=pltpu.VMEM),
        out_shape=jax.ShapeDtypeStruct((m, width), dtype),
        scratch_shapes=[
            pltpu.VMEM((slots, tile, k), BF16),
            pltpu.VMEM((k, width), BF16),
            pltpu.SemaphoreType.DMA((slots,)),
            pltpu.SemaphoreType.DMA,
        ],
        compiler_params=pltpu.CompilerParams(vmem_limit_bytes=VMEM),
        cost_estimate=pl.CostEstimate(
            flops=2 * m * k * width, bytes_accessed=2 * m * k, transcendentals=0
        ),
    )(a, x)


def add_columns(a, parts, chunks, total):
    m, k = a.shape
    rows, width = parts[0].shape
    count = len(parts)
    tile = min(m, 512)

    def kernel(chunks_ref, a_ref, *refs):
        out_ref = refs[-1]

        @pl.loop(0, m // tile)
        def _(i):
            at = pl.ds(pl.multiple_of(i * tile, tile), tile)
            acc = jnp.zeros((tile, width), F32) if total is None else refs[count][at, :]
            for j in range(count):
                cols = pl.ds(pl.multiple_of(chunks_ref[j] * rows, rows), rows)
                acc = acc + matmul(a_ref[at, cols], refs[j][...])
            out_ref[at, :] = acc

    extra = [] if total is None else [total]
    return pl.pallas_call(
        kernel,
        in_specs=[pl.BlockSpec(memory_space=pltpu.SMEM)]
        + [pl.BlockSpec(memory_space=pltpu.VMEM)] * (1 + count + len(extra)),
        out_specs=pl.BlockSpec(memory_space=pltpu.VMEM),
        out_shape=jax.ShapeDtypeStruct((m, width), F32),
        compiler_params=pltpu.CompilerParams(vmem_limit_bytes=RESIDENT),
        cost_estimate=pl.CostEstimate(
            flops=2 * m * rows * count * width, bytes_accessed=0, transcendentals=0
        ),
    )(jnp.stack(chunks).astype(jnp.int32), a, *parts, *extra)


def first_columns(a, parts, chunks):
    m, k = a.shape
    rows, width = parts[0].shape
    count = len(parts)

    def kernel(chunks_ref, a_ref, *refs):
        out_ref = refs[-1]
        for j in range(count):

            @pl.when(pl.program_id(0) == j)
            def _():
                part = matmul(a_ref[...], refs[j][...])
                out_ref[...] = part if j == 0 else part + out_ref[...]

    return pl.pallas_call(
        kernel,
        grid_spec=pltpu.PrefetchScalarGridSpec(
            num_scalar_prefetch=1,
            grid=(count,),
            in_specs=[pl.BlockSpec((m, rows), lambda i, chunks_ref: (0, chunks_ref[i]))]
            + [pl.BlockSpec((rows, width), lambda i, chunks_ref: (0, 0))] * count,
            out_specs=pl.BlockSpec((m, width), lambda i, chunks_ref: (0, 0)),
        ),
        out_shape=jax.ShapeDtypeStruct((m, width), F32),
        compiler_params=pltpu.CompilerParams(vmem_limit_bytes=VMEM),
        cost_estimate=pl.CostEstimate(
            flops=2 * m * rows * count * width,
            bytes_accessed=4 * m * rows * count,
            transcendentals=0,
        ),
    )(jnp.stack(chunks).astype(jnp.int32), a, *parts)


def gather_and_solve(a, own):
    depth = lax.axis_size("row")
    cores = lax.axis_size("col")
    z = lax.axis_index("row")
    c = lax.axis_index("col")
    rows = [own] + [
        lax.ppermute(own, "row", [(i, (i + d) % depth) for i in range(depth)])
        for d in range(1, depth)
    ]
    total = None
    step = max(depth // 2, 1)
    for first in range(0, depth, step):
        parts, chunks = [], []
        if total is not None:
            rows[first:], total = lax.optimization_barrier((rows[first:], total))
        for d in range(first, min(first + step, depth)):
            for e in range(cores):
                part = rows[d]
                if e > 0:
                    part = lax.ppermute(part, "col", [(i, (i + e) % cores) for i in range(cores)])
                parts.append(part)
                chunks.append((z - d) % depth * cores + (c - e) % cores)
        if total is None:
            total = first_columns(a, parts, chunks)
        else:
            total = add_columns(a, parts, chunks, total)
    return total


def columns_t(a, x, depth, cores):
    k, m = a.shape
    rows = m // (depth * cores)
    width = x.shape[1]
    which = jnp.stack([lax.axis_index("col"), lax.axis_index("row")]).astype(jnp.int32)

    def kernel(which_ref, a_ref, x_ref, out_ref):
        @pl.loop(0, cores * depth)
        def _(i):
            core = lax.rem(which_ref[0] + 1 + lax.div(i, depth), cores)
            z = lax.rem(which_ref[1] + i, depth)
            cols = pl.ds(pl.multiple_of((z * cores + core) * rows, rows), rows)
            out_ref[i] = matmul_t(a_ref[:, cols], x_ref[...]).astype(BF16)

    out = pl.pallas_call(
        kernel,
        in_specs=[pl.BlockSpec(memory_space=pltpu.SMEM)]
        + [pl.BlockSpec(memory_space=pltpu.VMEM)] * 2,
        out_specs=pl.BlockSpec(memory_space=pltpu.VMEM),
        out_shape=jax.ShapeDtypeStruct((cores * depth, rows, width), BF16),
        compiler_params=pltpu.CompilerParams(vmem_limit_bytes=RESIDENT),
        cost_estimate=pl.CostEstimate(
            flops=2 * k * m * width, bytes_accessed=0, transcendentals=0
        ),
    )(which, a, x)
    return out.reshape(cores, depth, rows, width)


def dot_t(a, x, first, count, tile, dtype):
    k = a.shape[0]
    width = x.shape[1]

    def kernel(a_ref, x_ref, *out_refs):
        part = matmul_t(a_ref[...], x_ref[...]).astype(dtype)
        for j, out_ref in enumerate(out_refs):

            @pl.when(pl.program_id(0) == j)
            def _():
                out_ref[...] = part

    return pl.pallas_call(
        kernel,
        grid=(count,),
        in_specs=[
            pl.BlockSpec((k, tile), lambda i: (0, first + i)),
            pl.BlockSpec((k, width), lambda i: (0, 0)),
        ],
        out_specs=[pl.BlockSpec((tile, width), lambda i: (0, 0))] * count,
        out_shape=[jax.ShapeDtypeStruct((tile, width), dtype)] * count,
        compiler_params=pltpu.CompilerParams(vmem_limit_bytes=VMEM),
        cost_estimate=pl.CostEstimate(
            flops=2 * k * count * tile * width,
            bytes_accessed=2 * k * count * tile,
            transcendentals=0,
        ),
    )(a, x)


def matmul_t_tiled(a, x):
    k, m = a.shape
    width = x.shape[1]
    tile = min(m, 1024)

    def kernel(a_ref, x_ref, out_ref):
        out_ref[...] = matmul_t(a_ref[...], x_ref[...]).astype(BF16)

    return pl.pallas_call(
        kernel,
        grid=(m // tile,),
        in_specs=[
            pl.BlockSpec((k, tile), lambda i: (0, i)),
            pl.BlockSpec((k, width), lambda i: (0, 0)),
        ],
        out_specs=pl.BlockSpec((tile, width), lambda i: (i, 0)),
        out_shape=jax.ShapeDtypeStruct((m, width), BF16),
        compiler_params=pltpu.CompilerParams(vmem_limit_bytes=VMEM),
        cost_estimate=pl.CostEstimate(
            flops=2 * k * m * width, bytes_accessed=2 * k * m, transcendentals=0
        ),
    )(a, x)


def solve_and_scatter(a, x):
    depth = lax.axis_size("row")
    cores = lax.axis_size("col")
    parts = columns_t(a, x, depth, cores)
    summed = parts[-1]
    for e in range(cores - 1):
        summed = summed + lax.ppermute(
            parts[e], "col", [(i, (i + 1 + e) % cores) for i in range(cores)]
        )
    total = summed[0].astype(F32)
    for d in range(1, depth):
        moved = lax.ppermute(summed[d], "row", [(j, (j + d) % depth) for j in range(depth)])
        total = total + moved.astype(F32)
    return total.astype(BF16)


def solve_and_sum_rows(inverse, x):
    depth = lax.axis_size("row")
    if depth != 4:
        return lax.psum(matmul_t(inverse, x), "row").astype(BF16)
    width = inverse.shape[1]
    size = width // CHUNKS
    z = lax.axis_index("row")
    inner = (z == 1) | (z == 2)
    ends = [(0, 1), (1, 0), (2, 3), (3, 2)]
    middle = [(1, 2), (2, 1)]

    def group(first, x):
        return dot_t(inverse, x, first, sizes.pop(0), size, BF16)

    total = jnp.zeros((width, x.shape[1]), BF16)
    sizes = list(GROUPS)
    own, outer_got, middle_got = list(group(0, x)), [], []
    for step in range(CHUNKS + 4):
        late = step - 4
        if late >= 0 and step < CHUNKS:
            send = jnp.where(inner, own[late] + middle_got[late], own[step])
        elif late >= 0:
            send = own[late] + middle_got[late]
        else:
            send = own[step]
        mid = step - 2
        if 0 <= mid < CHUNKS:
            both = own[mid] + outer_got[mid]
            send, both, outer_got[mid] = lax.optimization_barrier((send, both, outer_got[mid]))
            middle_got.append(lax.ppermute(both, "row", middle))
        if len(own) < CHUNKS and step >= len(own) - 3:
            x, send = lax.optimization_barrier((x, send))
            own.extend(group(len(own), x))
        outer_got.append(lax.ppermute(send, "row", ends))
        if late >= 0:
            others = jnp.where(
                inner,
                outer_got[late].astype(F32) + middle_got[late].astype(F32),
                outer_got[step].astype(F32),
            )
            done = (own[late].astype(F32) + others).astype(BF16)
            total = lax.dynamic_update_slice_in_dim(total, done, late * size, 0)
    return total


def slots_of(row_map, own, devices, depth):
    blocks = row_map.reshape(depth, -1)
    size = blocks.shape[1]
    cap = -(-size // devices)
    owner = blocks // own
    earlier = jnp.arange(size)[None, :] < jnp.arange(size)[:, None]
    rank = jnp.sum((owner[:, :, None] == owner[:, None, :]) & earlier[None], axis=2, dtype=jnp.int32)
    slot = owner * cap + rank
    hit = slot[:, None, :] == jnp.arange(devices * cap, dtype=jnp.int32)[None, :, None]
    local = jnp.max(jnp.where(hit, (blocks % own)[:, None, :], -1), axis=2)
    local = local.reshape(depth, devices, cap).transpose(1, 0, 2).reshape(devices, depth * cap)
    return hit.astype(BF16), local


def per_device(rhs_leaf, rhs_parent, inv_leaf, panel, row_map, inv_parent):
    leaves, depth, cores = (lax.axis_size(a) for a in ALL)
    devices = leaves * depth * cores
    me = lax.axis_index(ALL)
    own, width = rhs_parent.shape

    pick, local = slots_of(row_map[0], own, devices, depth)
    per_owner = local.shape[1]
    cap = per_owner // depth
    lists = gather_lists(local)
    mine = lax.dynamic_index_in_dim(lists, me, 2, keepdims=False).reshape(-1)
    place = (mine[None, :] == jnp.arange(own, dtype=jnp.int32)[:, None]).astype(BF16)

    forward = sum_cores(matmul_streamed(inv_leaf[0], rhs_leaf[0], BF16)).astype(BF16)
    update = matmul_streamed(panel[0], forward, BF16).reshape(depth, -1, width)
    packed = jnp.einsum("bsi,bir->bsr", pick, update, preferred_element_type=F32).astype(BF16)
    packed = packed.reshape(depth, devices, cap, width).transpose(1, 0, 2, 3)
    packed = packed.reshape(devices * per_owner, width)

    arrived = lax.all_to_all(packed, ALL, 0, 0, tiled=True)
    arrived = arrived.reshape(leaves, depth, cores * per_owner, width).astype(F32).sum(1)
    arrived = arrived.reshape(leaves * cores * per_owner, width).astype(BF16)
    reduced = (rhs_parent.astype(F32) - matmul(place, arrived)).astype(BF16)

    part = gather_and_solve(inv_parent, reduced)
    halves = swap_leaves(jnp.split(part, 2, axis=0), slice(0, None))
    fwd_parent = jnp.concatenate(halves, axis=0).astype(BF16)
    sol_parent = solve_and_scatter(inv_parent, fwd_parent)

    wanted = matmul_t(place, sol_parent).astype(BF16)
    wanted = wanted.reshape(leaves, 1, cores * per_owner, width)
    wanted = jnp.broadcast_to(wanted, (leaves, depth, cores * per_owner, width))
    got = lax.all_to_all(wanted.reshape(devices * per_owner, width), ALL, 0, 0, tiled=True)
    got = got.reshape(devices, depth, cap, width).transpose(1, 0, 2, 3)
    got = got.reshape(depth, devices * cap, width)
    picked = jnp.einsum("bsi,bsr->bir", pick, got, preferred_element_type=F32).astype(BF16)
    picked = picked.reshape(panel.shape[1], width)

    coupling = sum_cores(matmul_t_tiled(panel[0], picked))
    corrected = (forward.astype(F32) - coupling).astype(BF16)
    sol_leaf = solve_and_sum_rows(inv_leaf[0], corrected)
    return (sol_leaf[None], sol_parent)


def solution(mesh):
    in_specs = (
        P("leaf", "col", None),
        P(("leaf", "row", "col"), None),
        P("leaf", "row", "col"),
        P("leaf", "col", "row"),
        P("leaf", "col"),
        P(("row", "col"), "leaf"),
    )
    out_specs = (P("leaf", "col", None), P(("leaf", "row", "col"), None))
    return jax.shard_map(
        per_device, mesh=mesh, in_specs=in_specs, out_specs=out_specs, check_vma=False
    )
```
